512 devices in a mesh: boxes: 64 (over y, z), grp: 8 (over x, core).
Axes of the slice: x: 4, y: 8, z: 8, core: 2. Of those that a mesh axis runs over, the one named last changes fastest.
Arguments:
- densities: bfloat16 [1024, 256, 512], P(('boxes', 'grp')), may hold values from -6 to 6
- basis_source: bfloat16 [1024, 64, 256], P(('boxes', 'grp')), may hold values from -0.375 to 0.375
- basis_target: bfloat16 [1024, 64, 256], P(('boxes', 'grp')), may hold values from -0.75 to 0.75
- near_blocks: bfloat16 [1024, 256, 2048], P(('boxes', 'grp')), may hold values from -0.125 to 0.125
- near_leaves: int32 [1024, 8], P(('boxes', 'grp')), may hold values from 0 to 1023, as said below
- near_count: int32 [1024], P(('boxes', 'grp')), may hold values from 1 to 8
- far_coupling: bfloat16 [1024, 64, 2560], P(('boxes', 'grp')), may hold values from -0.125 to 0.125
- far_leaves: int32 [1024, 40], P(('boxes', 'grp')), may hold values from 0 to 1023, as said below
- far_count: int32 [1024], P(('boxes', 'grp')), may hold values from 1 to 40
- leaf_transfer: bfloat16 [1024, 64, 64], P(('boxes', 'grp')), may hold values from -0.375 to 0.375
- box_transfer: bfloat16 [64, 64, 64], replicated, may hold values from -0.375 to 0.375
- box_coupling: bfloat16 [64, 64, 1024], P('boxes'), may hold values from -0.1875 to 0.1875
- box_partners: int32 [64, 16], P('boxes'), may hold values from 0 to 63
- top_coupling: bfloat16 [8, 64, 256], replicated, may hold values from -0.375 to 0.375
- top_partners: int32 [8, 4], replicated, may hold values from 0 to 7
Outputs:
- potential: bfloat16 [1024, 256, 512], P(('boxes', 'grp'))
The draws below stay inside these ranges and needn't reach their ends.
Inputs may be any that keep to these rules, and one draw needn't show every extreme that they name: `near_leaves`: entry 0 of row t is t itself; every entry s of row t satisfies |s // 2 - t // 2| <= 1, and that distance is reached. `far_leaves`: every entry s of row t satisfies |s // 16 - t // 16| <= 1, and that distance is reached.
All inputs are finite; a program needn't handle non-finite values.
Results may differ from the reference program's by a relative error of at most 0.012.
Values may be sent and summed in bfloat16 or wider, within the bound.
No kernel may reach another device: no remote copies, remote signals or barrier semaphores. Data moves between devices by JAX's collectives and lax.ppermute only.
A program may use at most 64 MiB of HBM per device.

```python
import jax
import jax.numpy as jnp
from jax import lax

POINTS = 256
RANK = 64
VECTORS = 512
LEAF_DEV = 2
NEAR = 8
FAR_LEAF = 40
FAR_BOX = 16
FAR_TOP = 4
NEAR_REACH = 1
FAR_REACH = 1
CHILDREN = 8
GROUP_LEAVES = 16
BOXES = 64
TOPS = 8
LEAVES = 1024


def draw_near_leaves(key, part):
    key = jax.random.fold_in(key, 21)
    key_offset, key_slot = jax.random.split(key)
    leaf_ids = jnp.arange(LEAVES, dtype=jnp.int32)[:, None]
    holder_base = leaf_ids // LEAF_DEV
    devices = LEAVES // LEAF_DEV
    slot_ids = jnp.arange(NEAR, dtype=jnp.int32)[None, :]
    offset = jax.random.randint(key_offset, (LEAVES, NEAR), -NEAR_REACH, NEAR_REACH + 1, dtype=jnp.int32)
    far_side = jnp.where(holder_base + NEAR_REACH < devices, NEAR_REACH, -NEAR_REACH)
    offset = jnp.where(slot_ids == 1, far_side, offset)
    holder = jnp.clip(holder_base + offset, 0, devices - 1)
    within = jax.random.randint(key_slot, (LEAVES, NEAR), 0, LEAF_DEV, dtype=jnp.int32)
    chosen = holder * LEAF_DEV + within
    return jnp.where(slot_ids == 0, leaf_ids, chosen).astype(jnp.int32)


def draw_near_count(key, part):
    key = jax.random.fold_in(key, 22)
    counts = jax.random.randint(key, (LEAVES,), 1, NEAR + 1, dtype=jnp.int32)
    leaf_ids = jnp.arange(LEAVES, dtype=jnp.int32)
    return jnp.where(leaf_ids % LEAF_DEV == 0, NEAR, counts).astype(jnp.int32)


def draw_far_leaves(key, part):
    key = jax.random.fold_in(key, 23)
    key_offset, key_slot = jax.random.split(key)
    leaf_ids = jnp.arange(LEAVES, dtype=jnp.int32)[:, None]
    home_box = leaf_ids // GROUP_LEAVES
    slot_ids = jnp.arange(FAR_LEAF, dtype=jnp.int32)[None, :]
    offset = jax.random.randint(key_offset, (LEAVES, FAR_LEAF), -FAR_REACH, FAR_REACH + 1, dtype=jnp.int32)
    far_side = jnp.where(home_box + FAR_REACH < BOXES, FAR_REACH, -FAR_REACH)
    offset = jnp.where(slot_ids == 0, far_side, offset)
    source_box = jnp.clip(home_box + offset, 0, BOXES - 1)
    within = jax.random.randint(key_slot, (LEAVES, FAR_LEAF), 0, GROUP_LEAVES, dtype=jnp.int32)
    return (source_box * GROUP_LEAVES + within).astype(jnp.int32)


def draw_far_count(key, part):
    key = jax.random.fold_in(key, 24)
    counts = jax.random.randint(key, (LEAVES,), 1, FAR_LEAF + 1, dtype=jnp.int32)
    leaf_ids = jnp.arange(LEAVES, dtype=jnp.int32)
    return jnp.where(leaf_ids % LEAF_DEV == 0, FAR_LEAF, counts).astype(jnp.int32)


def set_ends(entries, stream_key, least, top_value):
    dims = entries.shape
    spot = [jax.random.randint(jax.random.fold_in(stream_key, axis), (), 0, dims[axis]) for axis in range(len(dims))]
    entries = entries.at[tuple(spot)].set(least)
    longest = dims.index(max(dims))
    spot[longest] = (spot[longest] + 1) % dims[longest]
    return entries.at[tuple(spot)].set(top_value)


def levels(stream_key, extent, shards, low, high):
    def one(axis_at, blocks):
        steps = jax.random.uniform(jax.random.fold_in(jax.random.fold_in(stream_key, 6), axis_at), (blocks,), jnp.float32, low / len(shards), high / len(shards))
        return jnp.repeat(jnp.exp(steps), extent[axis_at] // blocks).reshape((-1,) + (1,) * (len(extent) - axis_at - 1))

    level = one(*shards[0])
    for cut in shards[1:]:
        level = level * one(*cut)
    return level


def noise(key, dims, width, limit, pieces=(), kind=jnp.bfloat16):
    entries = width * jax.random.normal(key, dims, jnp.float32)
    if pieces:
        entries = entries * levels(key, dims, pieces, -0.22, 0.18)
    return jnp.clip(entries, -limit, limit).astype(kind)


def setup_inputs(seed: int = 0) -> dict:
    streams_of = jax.random.split(jax.random.key(seed), 16)
    return {
        "densities": noise(streams_of[0], (LEAVES, POINTS, VECTORS), 1.0, 6.0, ((0, 512),)),
        "basis_source": noise(streams_of[1], (LEAVES, RANK, POINTS), POINTS ** -0.5, 0.375, ((0, 512),)),
        "basis_target": noise(streams_of[2], (LEAVES, RANK, POINTS), RANK ** -0.5, 0.75, ((0, 512),)),
        "near_blocks": noise(streams_of[3], (LEAVES, POINTS, NEAR * POINTS), (NEAR * POINTS) ** -0.5, 0.125, ((0, 512),)),
        "near_leaves": draw_near_leaves(jax.random.fold_in(streams_of[15], 71), 0),
        "near_count": draw_near_count(jax.random.fold_in(streams_of[15], 71), 0),
        "far_coupling": noise(streams_of[6], (LEAVES, RANK, FAR_LEAF * RANK), (FAR_LEAF * RANK) ** -0.5, 0.125, ((0, 512),)),
        "far_leaves": draw_far_leaves(jax.random.fold_in(streams_of[15], 71), 0),
        "far_count": draw_far_count(jax.random.fold_in(streams_of[15], 71), 0),
        "leaf_transfer": noise(streams_of[9], (LEAVES, RANK, RANK), (4 * RANK) ** -0.5, 0.375, ((0, 512),)),
        "box_transfer": noise(streams_of[10], (BOXES, RANK, RANK), (4 * RANK) ** -0.5, 0.375),
        "box_coupling": noise(streams_of[11], (BOXES, RANK, FAR_BOX * RANK), (FAR_BOX * RANK) ** -0.5, 0.1875, ((0, 64),)),
        "box_partners": set_ends(jax.random.randint(streams_of[12], (BOXES, FAR_BOX), 0, BOXES), jax.random.fold_in(streams_of[12], 1), 0, BOXES - 1).astype(jnp.int32),
        "top_coupling": noise(streams_of[13], (TOPS, RANK, FAR_TOP * RANK), (FAR_TOP * RANK) ** -0.5, 0.375),
        "top_partners": set_ends(jax.random.randint(streams_of[14], (TOPS, FAR_TOP), 0, TOPS), jax.random.fold_in(streams_of[14], 1), 0, TOPS - 1).astype(jnp.int32),
    }


def product_pair(operands):
    return jnp.dot(operands[0], operands[1], preferred_element_type=jnp.float32)


def reference(densities, basis_source, basis_target, near_blocks, near_leaves, near_count, far_coupling, far_leaves, far_count, leaf_transfer, box_transfer, box_coupling, box_partners, top_coupling, top_partners):
    skeleton = lax.map(product_pair, (basis_source, densities)).astype(jnp.bfloat16)
    upward = lax.map(product_pair, (leaf_transfer, skeleton))
    box_skeleton = upward.reshape(BOXES, GROUP_LEAVES, RANK, VECTORS).sum(axis=1).astype(jnp.bfloat16)
    children = lax.map(product_pair, (box_transfer, box_skeleton))
    top_skeleton = children.reshape(TOPS, CHILDREN, RANK, VECTORS).sum(axis=1).astype(jnp.bfloat16)

    def top_row(operands):
        coupling, chosen = operands
        stacked = jnp.take(top_skeleton, chosen, axis=0).reshape(FAR_TOP * RANK, VECTORS)
        return jnp.dot(coupling, stacked, preferred_element_type=jnp.float32)

    top_local = lax.map(top_row, (top_coupling, top_partners)).astype(jnp.bfloat16)

    def box_row(operands):
        box_id, coupling, chosen, transfer = operands
        stacked = jnp.take(box_skeleton, chosen, axis=0).reshape(FAR_BOX * RANK, VECTORS)
        parent_local = top_local[(box_id // CHILDREN).astype(jnp.int32)]
        value = jnp.dot(coupling, stacked, preferred_element_type=jnp.float32)
        value = value + jnp.dot(transfer.T, parent_local, preferred_element_type=jnp.float32)
        return value.astype(jnp.bfloat16)

    box_ids = jnp.arange(BOXES, dtype=jnp.int32)
    box_local = lax.map(box_row, (box_ids, box_coupling, box_partners, box_transfer))

    near_slots = jnp.arange(NEAR, dtype=jnp.int32)
    far_slots = jnp.arange(FAR_LEAF, dtype=jnp.int32)

    def finish(operands):
        leaf_id, near_block, near_pick, near_used, coupling, far_pick, far_used, transfer, target = operands
        far_rows = jnp.take(skeleton, far_pick, axis=0)
        far_rows = jnp.where((far_slots < far_used)[:, None, None], far_rows, jnp.zeros((), far_rows.dtype))
        far_field = jnp.dot(coupling, far_rows.reshape(FAR_LEAF * RANK, VECTORS), preferred_element_type=jnp.float32)
        parent_local = box_local[(leaf_id // GROUP_LEAVES).astype(jnp.int32)]
        leaf_local = (far_field + jnp.dot(transfer.T, parent_local, preferred_element_type=jnp.float32)).astype(jnp.bfloat16)
        near_rows = jnp.take(densities, near_pick, axis=0)
        near_rows = jnp.where((near_slots < near_used)[:, None, None], near_rows, jnp.zeros((), near_rows.dtype))
        near_field = jnp.dot(near_block, near_rows.reshape(NEAR * POINTS, VECTORS), preferred_element_type=jnp.float32)
        result = jnp.dot(target.T, leaf_local, preferred_element_type=jnp.float32) + near_field
        return result.astype(jnp.bfloat16)

    leaf_ids = jnp.arange(LEAVES, dtype=jnp.int32)
    return lax.map(finish, (leaf_ids, near_blocks, near_leaves, near_count, far_coupling, far_leaves, far_count, leaf_transfer, basis_target))
```

```python
import functools

import jax
import jax.numpy as jnp
from jax import lax
from jax.experimental import pallas as pl
from jax.experimental.pallas import tpu as pltpu
from jax.sharding import Mesh, PartitionSpec as P

RANK = 64
CHILDREN = 8
F32 = jnp.float32
BF16 = jnp.bfloat16
VMEM = pltpu.VMEM
SMEM = pltpu.SMEM


def dot(a, b):
    return jnp.dot(a, b, preferred_element_type=F32)


def dot_t(a, b):
    return lax.dot_general(a, b, (((0,), (0,)), ((), ())), preferred_element_type=F32)


def call(body, out_shape, spaces, flops, moved, scratch=(), limit=32 << 20):
    outs = jax.tree.map(lambda _: pl.BlockSpec(memory_space=VMEM), out_shape)
    return pl.pallas_call(
        body,
        out_shape=out_shape,
        in_specs=[pl.BlockSpec(memory_space=s) for s in spaces],
        out_specs=outs,
        scratch_shapes=list(scratch),
        compiler_params=pltpu.CompilerParams(vmem_limit_bytes=limit),
        cost_estimate=pl.CostEstimate(flops=flops, bytes_accessed=moved, transcendentals=0),
    )


def upward_body(groups, basis, densities, transfer, skeleton, pieces):
    total = None
    for leaf in range(densities.shape[0]):
        value = dot(basis[leaf], densities[leaf]).astype(BF16)
        skeleton[leaf] = value
        term = dot(transfer[leaf], value)
        total = term if total is None else total + term
    total = total.astype(BF16)
    rows, cols = pieces.shape[1:]
    for piece in range(groups):
        top, left = (piece % 2) * rows, (piece // 2) * cols
        pieces[piece] = total[top : top + rows, left : left + cols]


def spread_body(arrived, copies):
    total = arrived[0].astype(F32)
    for piece in range(1, arrived.shape[0]):
        total = total + arrived[piece].astype(F32)
    total = total.astype(BF16)
    for target in range(copies.shape[0]):
        copies[target] = total


def weight_body(coupling, transfer, top_coupling, top_partners, weights):
    box = lax.axis_index("boxes")
    half = lax.axis_index("core")
    parent = box // CHILDREN
    own = transfer[box]
    lefts = dot_t(own, top_coupling[parent])
    near = coupling.shape[-1]

    def keep(value):
        lane = lax.broadcasted_iota(jnp.int32, value.shape, 1)
        return jnp.where((lane // (RANK // 2)) % 2 == half, value, 0.0).astype(BF16)

    weights[:, :near] = keep(coupling[0].astype(F32))
    span = CHILDREN * RANK
    for slot in range(top_partners.shape[1]):
        top = top_partners[parent, slot]
        left = lefts[:, slot * RANK : (slot + 1) * RANK].astype(BF16)
        wide = jnp.concatenate([dot(left, transfer[top * CHILDREN + k]) for k in range(CHILDREN)], axis=1)
        weights[:, near + slot * span : near + (slot + 1) * span] = keep(wide)


def box_body(weights, boxes, box_partners, top_partners, copies):
    parent = lax.axis_index("boxes") // CHILDREN
    sources = [box_partners[0, j] for j in range(box_partners.shape[1])]
    for slot in range(top_partners.shape[1]):
        first = top_partners[parent, slot] * CHILDREN
        sources += [first + k for k in range(CHILDREN)]
    total = None
    step = 4
    for at in range(0, len(sources), step):
        rows = []
        for source in sources[at : at + step]:
            value = boxes[source]
            rows += [value, value]
        term = dot(weights[:, at * RANK : (at + step) * RANK], jnp.concatenate(rows, axis=0))
        total = term if total is None else total + term
    total = total.astype(BF16)
    for target in range(copies.shape[0]):
        copies[target] = total


def trio_body(behind, own, ahead, copies):
    for target in range(copies.shape[0]):
        copies[target, 0] = behind[...]
        copies[target, 1] = own[...]
        copies[target, 2] = ahead[...]


def near_body(device_of, blocks, behind, own, ahead, leaves, count, out, window, sems):
    loads = [
        pltpu.make_async_copy(part, window.at[pl.ds(2 * i, 2)], sems.at[i])
        for i, part in enumerate((behind, own, ahead))
    ]
    for load in loads:
        load.start()
    for load in loads:
        load.wait()
    base = (device_of() - 1) * own.shape[0]
    points = own.shape[1]
    for leaf in range(own.shape[0]):
        total = None
        for j in range(leaves.shape[1]):
            value = window[leaves[leaf, j] - base]
            value = jnp.where(j < count[leaf], value, jnp.zeros_like(value))
            term = dot(blocks[leaf, :, j * points : (j + 1) * points], value)
            total = term if total is None else total + term
        out[leaf] = total


def leaf_body(
    group_leaves, far_coupling, mine, other, far_leaves, far_count, local, transfer, target, near, out, window, sems
):
    half = lax.axis_index("core")
    loads = [
        pltpu.make_async_copy(mine, window.at[half], sems.at[0]),
        pltpu.make_async_copy(other, window.at[1 - half], sems.at[1]),
    ]
    for load in loads:
        load.start()
    parts = []
    for piece in range(0, local.shape[0], 2):
        parts.append(local[piece].astype(F32) + local[piece + 1].astype(F32))
    box_local = jnp.concatenate(parts, axis=1).astype(BF16)
    base = (lax.axis_index("boxes") - 1) * group_leaves
    for load in loads:
        load.wait()
    step = 4
    leaf_dev = transfer.shape[0]
    for leaf in range(leaf_dev):
        total = dot_t(transfer[leaf], box_local)
        for at in range(0, far_leaves.shape[1], step):
            rows = []
            for j in range(at, at + step):
                source = far_leaves[leaf, j] - base
                box, within = source // group_leaves, source % group_leaves
                chip, side, which = within // (2 * leaf_dev), (within // leaf_dev) % 2, within % leaf_dev
                value = window[side, chip, box, which]
                rows.append(jnp.where(j < far_count[leaf], value, jnp.zeros_like(value)))
            total = total + dot(
                far_coupling[leaf, :, at * RANK : (at + step) * RANK], jnp.concatenate(rows, axis=0)
            )
        out[leaf] = (dot_t(target[leaf], total.astype(BF16)) + near[leaf]).astype(BF16)


def shift(block, axis, distance):
    devices = range(lax.axis_size(axis))
    route = [(i - distance, i) for i in devices if i - distance in devices]
    return lax.ppermute(block, axis, route)


def shards(
    densities,
    basis_source,
    basis_target,
    near_blocks,
    near_leaves,
    near_count,
    far_coupling,
    far_leaves,
    far_count,
    leaf_transfer,
    box_transfer,
    box_coupling,
    box_partners,
    top_coupling,
    top_partners,
):
    chips, cores = lax.axis_size("x"), lax.axis_size("core")
    groups = chips * cores
    boxes = lax.axis_size("boxes")
    leaf_dev, points, vectors = densities.shape
    cols, rows = vectors // chips, RANK // cores
    grp = ("x", "core")
    line = ("boxes", "x", "core")

    skeleton, pieces = call(
        functools.partial(upward_body, groups),
        (
            jax.ShapeDtypeStruct((leaf_dev, RANK, vectors), BF16),
            jax.ShapeDtypeStruct((groups, rows, cols), BF16),
        ),
        [VMEM] * 3,
        2 * leaf_dev * RANK * vectors * (points + RANK),
        densities.size * 2,
    )(basis_source, densities, leaf_transfer)
    arrived = lax.all_to_all(pieces, grp, 0, 0, tiled=True)

    behind_skeleton = shift(skeleton, "boxes", 1)
    ahead_skeleton = shift(skeleton, "boxes", -1)

    spread = call(
        spread_body,
        jax.ShapeDtypeStruct((boxes, rows, cols), BF16),
        [VMEM],
        groups * rows * cols,
        boxes * rows * cols * 2,
    )(arrived)
    all_boxes = lax.all_to_all(spread, "boxes", 0, 0, tiled=True)

    trio = call(
        trio_body,
        jax.ShapeDtypeStruct((chips, 3, leaf_dev, RANK, vectors), BF16),
        [VMEM] * 3,
        0,
        chips * 3 * skeleton.size * 2,
    )(behind_skeleton, skeleton, ahead_skeleton)
    mine = lax.all_to_all(trio, "x", 0, 0, tiled=True)
    other = lax.ppermute(mine, "core", [(0, 1), (1, 0)])

    behind = shift(densities, line, 1)
    ahead = shift(densities, line, -1)

    sources = box_partners.shape[1] + top_partners.shape[1] * CHILDREN
    weights = call(
        weight_body,
        jax.ShapeDtypeStruct((RANK, sources * RANK), BF16),
        [VMEM, VMEM, VMEM, SMEM],
        2 * RANK * RANK * RANK * sources,
        box_transfer.size * 2,
    )(box_coupling, box_transfer, top_coupling, top_partners)
    local = call(
        box_body,
        jax.ShapeDtypeStruct((groups, RANK, cols), BF16),
        [VMEM, VMEM, SMEM, SMEM],
        2 * RANK * RANK * sources * cols,
        all_boxes.size * 2,
    )(weights, all_boxes, box_partners, top_partners)
    local = lax.all_to_all(local, grp, 0, 0, tiled=True)

    def device_of():
        return (lax.axis_index("boxes") * chips + lax.axis_index("x")) * cores + lax.axis_index("core")

    near_field = call(
        functools.partial(near_body, device_of),
        jax.ShapeDtypeStruct((leaf_dev, points, vectors), F32),
        [VMEM, pl.ANY, pl.ANY, pl.ANY, SMEM, SMEM],
        2 * near_blocks.size * vectors,
        near_blocks.size * 2 + 5 * densities.size * 2,
        (VMEM((3 * leaf_dev, points, vectors), BF16), pltpu.SemaphoreType.DMA((3,))),
    )(near_blocks, behind, densities, ahead, near_leaves, near_count)

    return call(
        functools.partial(leaf_body, groups * leaf_dev),
        jax.ShapeDtypeStruct(densities.shape, BF16),
        [VMEM, pl.ANY, pl.ANY, SMEM, SMEM, VMEM, VMEM, VMEM, VMEM],
        2 * far_coupling.size * vectors,
        2 * mine.size * 2 + 3 * densities.size * 2,
        (VMEM((2,) + mine.shape, BF16), pltpu.SemaphoreType.DMA((2,))),
    )(far_coupling, mine, other, far_leaves, far_count, local, leaf_transfer, basis_target, near_field)


def solution(mesh):
    boxes, groups = mesh.devices.shape
    fine = Mesh(mesh.devices.reshape(boxes, groups // 2, 2), ("boxes", "x", "core"))
    line = ("boxes", "x", "core")
    leaf = P(line, None, None)
    placed = (
        leaf,
        leaf,
        leaf,
        leaf,
        P(line, None),
        P(line),
        leaf,
        P(line, None),
        P(line),
        leaf,
        P(),
        P("boxes", None, None),
        P("boxes", None),
        P(),
        P(),
    )
    return jax.shard_map(shards, mesh=fine, in_specs=placed, out_specs=leaf, check_vma=False)
```

```python
import functools

import jax
import jax.numpy as jnp
from jax import lax
from jax.experimental import pallas as pl
from jax.experimental.pallas import tpu as pltpu
from jax.sharding import Mesh, PartitionSpec as P

RANK = 64
CHILDREN = 8
F32 = jnp.float32
BF16 = jnp.bfloat16
VMEM = pltpu.VMEM
SMEM = pltpu.SMEM
HBM = pltpu.HBM
WIDE = 119 << 19


def dot(a, b):
    return jnp.dot(a, b, preferred_element_type=F32)


def dot_t(a, b):
    return lax.dot_general(a, b, (((0,), (0,)), ((), ())), preferred_element_type=F32)


def call(body, out_shape, spaces, flops, moved, scratch=(), limit=32 << 20, out_space=VMEM):
    outs = jax.tree.map(lambda _: pl.BlockSpec(memory_space=out_space), out_shape)
    return pl.pallas_call(
        body,
        out_shape=out_shape,
        in_specs=[pl.BlockSpec(memory_space=s) for s in spaces],
        out_specs=outs,
        scratch_shapes=list(scratch),
        compiler_params=pltpu.CompilerParams(vmem_limit_bytes=limit),
        cost_estimate=pl.CostEstimate(flops=flops, bytes_accessed=moved, transcendentals=0),
    )


def load_all(sources, places, sems):
    loads = [pltpu.make_async_copy(a, b, sems.at[i]) for i, (a, b) in enumerate(zip(sources, places))]
    for load in loads:
        load.start()
    return loads


def upward_body(groups, basis_far, densities_far, transfer_far, skeleton, pieces, basis, densities, transfer, sems):
    for load in load_all((basis_far, densities_far, transfer_far), (basis, densities, transfer), sems):
        load.wait()
    total = None
    for leaf in range(densities.shape[0]):
        value = dot(basis[leaf], densities[leaf]).astype(BF16)
        skeleton[leaf] = value
        term = dot(transfer[leaf], value)
        total = term if total is None else total + term
    total = total.astype(BF16)
    rows, cols = pieces.shape[1:]
    for piece in range(groups):
        top, left = (piece % 2) * rows, (piece // 2) * cols
        pieces[piece] = total[top : top + rows, left : left + cols]


def spread_body(arrived, even, own, odd, copies, joined):
    joined[0] = even[...]
    joined[1] = own[...]
    joined[2] = odd[...]
    total = arrived[0].astype(F32)
    for piece in range(1, arrived.shape[0]):
        total = total + arrived[piece].astype(F32)
    total = total.astype(BF16)
    for target in range(copies.shape[0]):
        copies[target] = total


def weight_body(coupling_far, transfer_far, top_far, top_partners, weights, coupling, own, row, transfer, sems):
    box = lax.axis_index("boxes")
    half = lax.axis_index("core")
    parent = box // CHILDREN
    slots = top_partners.shape[0]
    sources = [coupling_far.at[0], transfer_far.at[box], top_far.at[parent]]
    sources += [transfer_far.at[pl.ds(top_partners[slot, parent] * CHILDREN, CHILDREN)] for slot in range(slots)]
    loads = load_all(sources, [coupling, own, row] + [transfer.at[slot] for slot in range(slots)], sems)
    for load in loads:
        load.wait()
    lefts = dot_t(own[...], row[...])
    near = coupling.shape[-1]

    def keep(value):
        lane = lax.broadcasted_iota(jnp.int32, value.shape, 1)
        return jnp.where((lane // (RANK // 2)) % 2 == half, value, 0.0).astype(BF16)

    weights[:, :near] = keep(coupling[...].astype(F32))
    span = CHILDREN * RANK
    for slot in range(slots):
        left = lefts[:, slot * RANK : (slot + 1) * RANK].astype(BF16)
        wide = jnp.concatenate([dot(left, transfer[slot, k]) for k in range(CHILDREN)], axis=1)
        weights[:, near + slot * span : near + (slot + 1) * span] = keep(wide)


def box_body(weights, boxes, box_partners, top_partners, copies):
    parent = lax.axis_index("boxes") // CHILDREN
    sources = [box_partners[0, j] for j in range(box_partners.shape[1])]
    for slot in range(top_partners.shape[0]):
        first = top_partners[slot, parent] * CHILDREN
        sources += [first + k for k in range(CHILDREN)]
    total = None
    step = 4
    for at in range(0, len(sources), step):
        rows = []
        for source in sources[at : at + step]:
            value = boxes[source]
            rows += [value, value]
        term = dot(weights[:, at * RANK : (at + step) * RANK], jnp.concatenate(rows, axis=0))
        total = term if total is None else total + term
    total = total.astype(BF16)
    for target in range(copies.shape[0]):
        copies[target] = total


def place(offset, index):
    return jnp.where(index % 2 == 1, offset, 2 - offset)


def near_body(device_of, blocks, even, own, odd, leaves, count, out, window, sems):
    leaf_dev, points, _ = own.shape
    blank = 3 * leaf_dev
    places = [window.at[pl.ds(i * leaf_dev, leaf_dev)] for i in range(3)]
    loads = load_all((even, own, odd), places, sems)
    window[blank] = jnp.zeros(window.shape[1:], BF16)
    device = device_of()
    base = (device - 1) * leaf_dev
    for load in loads:
        load.wait()
    for leaf in range(leaf_dev):
        total = None
        for j in range(leaves.shape[1]):
            source = leaves[leaf, j] - base
            at = place(source // leaf_dev, device) * leaf_dev + source % leaf_dev
            value = window[jnp.where(j < count[leaf], at, blank)]
            term = dot(blocks[leaf, :, j * points : (j + 1) * points], value)
            total = term if total is None else total + term
        out[leaf] = total


def leaf_body(
    group_leaves,
    coupling_far,
    skeletons_far,
    near_far,
    transfer,
    target,
    far_leaves,
    far_count,
    local,
    out,
    coupling,
    skeletons,
    near,
    sems,
):
    box_of = lax.axis_index("boxes")
    leaf_dev = transfer.shape[0]
    blank = skeletons.shape[0] - 1
    loads = load_all(
        (coupling_far, skeletons_far, near_far), (coupling, skeletons.at[pl.ds(0, blank)], near), sems
    )
    skeletons[blank] = jnp.zeros(skeletons.shape[1:], BF16)
    parts = []
    for piece in range(0, local.shape[0], 2):
        parts.append(local[piece].astype(F32) + local[piece + 1].astype(F32))
    box_local = jnp.concatenate(parts, axis=1).astype(BF16)
    base = (box_of - 1) * group_leaves
    step = 4
    for load in loads[:2]:
        load.wait()
    for leaf in range(leaf_dev):
        total = dot_t(transfer[leaf], box_local)
        for at in range(0, far_leaves.shape[1], step):
            rows = []
            for j in range(at, at + step):
                source = far_leaves[leaf, j] - base
                within = source % group_leaves
                spot = place(source // group_leaves, box_of) * leaf_dev + within % leaf_dev
                spot = (within // leaf_dev) * 3 * leaf_dev + spot
                rows.append(skeletons[jnp.where(j < far_count[leaf], spot, blank)])
            total = total + dot(
                coupling[leaf, :, at * RANK : (at + step) * RANK], jnp.concatenate(rows, axis=0)
            )
        if leaf == 0:
            loads[2].wait()
        out[leaf] = (dot_t(target[leaf], total.astype(BF16)) + near[leaf]).astype(BF16)


def swap(block, axis, first):
    size = lax.axis_size(axis)
    pairs = [(i, i + 1) for i in range(first, size - 1, 2)]
    return lax.ppermute(block, axis, pairs + [(b, a) for a, b in pairs])


def shards(
    densities,
    basis_source,
    basis_target,
    near_blocks,
    near_leaves,
    near_count,
    far_coupling,
    far_leaves,
    far_count,
    leaf_transfer,
    box_transfer,
    box_coupling,
    box_partners,
    top_coupling,
    top_partners,
):
    chips, cores = lax.axis_size("x"), lax.axis_size("core")
    groups = chips * cores
    boxes = lax.axis_size("boxes")
    leaf_dev, points, vectors = densities.shape
    cols, rows = vectors // chips, RANK // cores
    grp = ("x", "core")
    line = ("boxes", "x", "core")

    skeleton, pieces = call(
        functools.partial(upward_body, groups),
        (
            jax.ShapeDtypeStruct((leaf_dev, RANK, vectors), BF16),
            jax.ShapeDtypeStruct((groups, rows, cols), BF16),
        ),
        [HBM] * 3,
        2 * leaf_dev * RANK * vectors * (points + RANK),
        densities.size * 2,
        (
            VMEM(basis_source.shape, BF16),
            VMEM(densities.shape, BF16),
            VMEM(leaf_transfer.shape, BF16),
            pltpu.SemaphoreType.DMA((3,)),
        ),
        WIDE,
    )(basis_source, densities, leaf_transfer)
    arrived = lax.all_to_all(pieces, grp, 0, 0, tiled=True)

    even_skeleton = swap(skeleton, "boxes", 0)
    odd_skeleton = swap(skeleton, "boxes", 1)

    spread, trio = call(
        spread_body,
        (
            jax.ShapeDtypeStruct((boxes, rows, cols), BF16),
            jax.ShapeDtypeStruct((3, leaf_dev, RANK, vectors), BF16),
        ),
        [VMEM] * 4,
        groups * rows * cols,
        boxes * rows * cols * 2,
    )(arrived, even_skeleton, skeleton, odd_skeleton)
    all_boxes = lax.all_to_all(spread, "boxes", 0, 0, tiled=True)
    window = lax.all_gather(trio, grp, axis=0, tiled=False)

    held, _ = lax.optimization_barrier((densities, spread))
    even = swap(held, line, 0)
    odd = swap(held, line, 1)

    tops = top_partners.T
    sources = box_partners.shape[1] + tops.shape[0] * CHILDREN
    weights = call(
        weight_body,
        jax.ShapeDtypeStruct((RANK, sources * RANK), BF16),
        [HBM, HBM, HBM, SMEM],
        2 * RANK * RANK * RANK * sources,
        box_transfer.size * 2,
        (
            VMEM(box_coupling.shape[1:], BF16),
            VMEM(box_transfer.shape[1:], BF16),
            VMEM(top_coupling.shape[1:], BF16),
            VMEM((tops.shape[0], CHILDREN) + box_transfer.shape[1:], BF16),
            pltpu.SemaphoreType.DMA((3 + tops.shape[0],)),
        ),
    )(box_coupling, box_transfer, top_coupling, tops)
    local = call(
        box_body,
        jax.ShapeDtypeStruct((groups, RANK, cols), BF16),
        [VMEM, VMEM, SMEM, SMEM],
        2 * RANK * RANK * sources * cols,
        all_boxes.size * 2,
    )(weights, all_boxes, box_partners, tops)
    local = lax.all_to_all(local, grp, 0, 0, tiled=True)

    def device_of():
        return (lax.axis_index("boxes") * chips + lax.axis_index("x")) * cores + lax.axis_index("core")

    near_field = call(
        functools.partial(near_body, device_of),
        jax.ShapeDtypeStruct((leaf_dev, points, vectors), F32),
        [VMEM] + [HBM] * 3 + [SMEM] * 2,
        2 * near_blocks.size * vectors,
        near_blocks.size * 2 + 5 * densities.size * 2,
        (
            VMEM((3 * leaf_dev + 1, points, vectors), BF16),
            pltpu.SemaphoreType.DMA((3,)),
        ),
    )(near_blocks, even, densities, odd, near_leaves, near_count)
    flat = window.reshape((groups * 3 * leaf_dev, RANK, vectors))
    return call(
        functools.partial(leaf_body, groups * leaf_dev),
        jax.ShapeDtypeStruct(densities.shape, BF16),
        [HBM] * 3 + [VMEM] * 2 + [SMEM] * 2 + [VMEM],
        2 * far_coupling.size * vectors,
        2 * window.size,
        (
            VMEM(far_coupling.shape, BF16),
            VMEM((flat.shape[0] + 1, RANK, vectors), BF16),
            VMEM(near_field.shape, F32),
            pltpu.SemaphoreType.DMA((3,)),
        ),
        WIDE,
    )(
        far_coupling,
        flat,
        near_field,
        leaf_transfer,
        basis_target,
        far_leaves,
        far_count,
        local,
    )


def solution(mesh):
    boxes, groups = mesh.devices.shape
    fine = Mesh(mesh.devices.reshape(boxes, groups // 2, 2), ("boxes", "x", "core"))
    line = ("boxes", "x", "core")
    leaf = P(line, None, None)
    placed = (
        leaf,
        leaf,
        leaf,
        leaf,
        P(line, None),
        P(line),
        leaf,
        P(line, None),
        P(line),
        leaf,
        P(),
        P("boxes", None, None),
        P("boxes", None),
        P(),
        P(),
    )
    return jax.shard_map(shards, mesh=fine, in_specs=placed, out_specs=leaf, check_vma=False)
```

```python
import functools

import jax
import jax.numpy as jnp
from jax import lax
from jax.experimental import pallas as pl
from jax.experimental.pallas import tpu as pltpu
from jax.sharding import Mesh, PartitionSpec as P

RANK = 64
CHILDREN = 8
F32 = jnp.float32
BF16 = jnp.bfloat16
VMEM = pltpu.VMEM
SMEM = pltpu.SMEM
HBM = pltpu.HBM
WIDE = 119 << 19
HUGE = 10**9


def dot(a, b):
    return jnp.dot(a, b, preferred_element_type=F32)


def dot_t(a, b):
    return lax.dot_general(a, b, (((0,), (0,)), ((), ())), preferred_element_type=F32)


def call(body, out_shape, spaces, flops, moved, scratch=(), limit=32 << 20, out_space=VMEM):
    outs = jax.tree.map(lambda _: pl.BlockSpec(memory_space=out_space), out_shape)
    return pl.pallas_call(
        body,
        out_shape=out_shape,
        in_specs=[pl.BlockSpec(memory_space=s) for s in spaces],
        out_specs=outs,
        scratch_shapes=list(scratch),
        compiler_params=pltpu.CompilerParams(vmem_limit_bytes=limit),
        cost_estimate=pl.CostEstimate(flops=flops, bytes_accessed=moved, transcendentals=0),
    )


def load_all(sources, places, sems):
    loads = [pltpu.make_async_copy(a, b, sems.at[i]) for i, (a, b) in enumerate(zip(sources, places))]
    for load in loads:
        load.start()
    return loads


def upward_body(groups, basis_far, densities_far, transfer_far, skeleton, pieces, basis, densities, transfer, sems):
    for load in load_all((basis_far, densities_far, transfer_far), (basis, densities, transfer), sems):
        load.wait()
    total = None
    for leaf in range(densities.shape[0]):
        value = dot(basis[leaf], densities[leaf]).astype(BF16)
        skeleton[leaf] = value
        term = dot(transfer[leaf], value)
        total = term if total is None else total + term
    total = total.astype(BF16)
    rows, cols = pieces.shape[1:]
    for piece in range(groups):
        top, left = (piece % 2) * rows, (piece // 2) * cols
        pieces[piece] = total[top : top + rows, left : left + cols]


def pair_body(first, second, joined):
    joined[0] = first[...]
    joined[1] = second[...]


def join_body(first, second, after, even, odd, joined):
    half = first.shape[0]
    joined[:half] = first[...]
    joined[half:] = second[...]


def spread_body(arrived, even, own, odd, before, copies, joined):
    joined[0] = even[...]
    joined[1] = own[...]
    joined[2] = odd[...]
    total = arrived[0].astype(F32)
    for piece in range(1, arrived.shape[0]):
        total = total + arrived[piece].astype(F32)
    total = total.astype(BF16)
    for target in range(copies.shape[0]):
        copies[target] = total


def weight_body(coupling_far, transfer_far, top_far, top_partners, weights, coupling, own, row, transfer, sems):
    box = lax.axis_index("boxes")
    half = lax.axis_index("core")
    parent = box // CHILDREN
    slots = top_partners.shape[0]
    sources = [coupling_far.at[0], transfer_far.at[box], top_far.at[parent]]
    sources += [transfer_far.at[pl.ds(top_partners[slot, parent] * CHILDREN, CHILDREN)] for slot in range(slots)]
    loads = load_all(sources, [coupling, own, row] + [transfer.at[slot] for slot in range(slots)], sems)
    for load in loads:
        load.wait()
    lefts = dot_t(own[...], row[...])
    near = coupling.shape[-1]

    def keep(value):
        lane = lax.broadcasted_iota(jnp.int32, value.shape, 1)
        return jnp.where((lane // (RANK // 2)) % 2 == half, value, 0.0).astype(BF16)

    weights[:, :near] = keep(coupling[...].astype(F32))
    span = CHILDREN * RANK
    for slot in range(slots):
        left = lefts[:, slot * RANK : (slot + 1) * RANK].astype(BF16)
        wide = jnp.concatenate([dot(left, transfer[slot, k]) for k in range(CHILDREN)], axis=1)
        weights[:, near + slot * span : near + (slot + 1) * span] = keep(wide)


def box_body(weights, boxes, box_partners, top_partners, copies):
    parent = lax.axis_index("boxes") // CHILDREN
    sources = [box_partners[0, j] for j in range(box_partners.shape[1])]
    for slot in range(top_partners.shape[0]):
        first = top_partners[slot, parent] * CHILDREN
        sources += [first + k for k in range(CHILDREN)]
    total = None
    step = 4
    for at in range(0, len(sources), step):
        rows = []
        for source in sources[at : at + step]:
            value = boxes[source]
            rows += [value, value]
        term = dot(weights[:, at * RANK : (at + step) * RANK], jnp.concatenate(rows, axis=0))
        total = term if total is None else total + term
    total = total.astype(BF16)
    for target in range(copies.shape[0]):
        copies[target] = total


def place(offset, index):
    return jnp.where(index % 2 == 1, offset, 2 - offset)


def near_body(
    device_of, blocks_far, even, own, odd, leaves_far, count_far, out_far, blocks, window, leaves, count, out, sems, out_sems
):
    leaf_dev, points, _ = own.shape
    blank = 3 * leaf_dev
    sources = [leaves_far, count_far, even, own, odd] + [blocks_far.at[leaf] for leaf in range(leaf_dev)]
    places = [leaves, count] + [window.at[pl.ds(i * leaf_dev, leaf_dev)] for i in range(3)]
    loads = load_all(sources, places + [blocks.at[leaf] for leaf in range(leaf_dev)], sems)
    window[blank] = jnp.zeros(window.shape[1:], BF16)
    device = device_of()
    base = (device - 1) * leaf_dev
    for load in loads[:5]:
        load.wait()
    stores = []
    for leaf in range(leaf_dev):
        loads[5 + leaf].wait()
        total = None
        for j in range(leaves.shape[1]):
            source = leaves[leaf, j] - base
            at = place(source // leaf_dev, device) * leaf_dev + source % leaf_dev
            value = window[jnp.where(j < count[leaf], at, blank)]
            term = dot(blocks[leaf, :, j * points : (j + 1) * points], value)
            total = term if total is None else total + term
        out[leaf] = total
        stores += load_all((out.at[leaf],), (out_far.at[leaf],), out_sems.at[pl.ds(leaf, 1)])
    for store in stores:
        store.wait()


def leaf_body(
    group_leaves,
    coupling_far,
    mine,
    other,
    near_far,
    transfer_far,
    target_far,
    far_leaves_far,
    far_count_far,
    local_far,
    out_far,
    coupling,
    skeletons,
    near,
    transfer,
    target,
    far_leaves,
    far_count,
    local,
    out,
    sems,
    out_sems,
):
    box_of = lax.axis_index("boxes")
    leaf_dev = transfer.shape[0]
    blank = skeletons.shape[0] - 1
    half = lax.axis_index("core")
    chip_of = lax.axis_index("x")
    loads = load_all(
        (far_leaves_far, far_count_far, local_far, transfer_far, coupling_far, mine, other, target_far, near_far),
        (
            far_leaves,
            far_count,
            local,
            transfer,
            coupling,
            skeletons.at[pl.ds(half * (blank // 2), blank // 2)],
            skeletons.at[pl.ds((1 - half) * (blank // 2), blank // 2)],
            target,
            near,
        ),
        sems,
    )
    skeletons[blank] = jnp.zeros(skeletons.shape[1:], BF16)
    for load in loads[:3]:
        load.wait()
    parts = []
    for piece in range(0, local.shape[0], 2):
        parts.append(local[piece].astype(F32) + local[piece + 1].astype(F32))
    box_local = jnp.concatenate(parts, axis=1).astype(BF16)
    base = (box_of - 1) * group_leaves
    step = 4
    for load in loads[3:7]:
        load.wait()
    stores = []
    for leaf in range(leaf_dev):
        total = dot_t(transfer[leaf], box_local)
        for at in range(0, far_leaves.shape[1], step):
            rows = []
            for j in range(at, at + step):
                source = far_leaves[leaf, j] - base
                within = source % group_leaves
                spot = place(source // group_leaves, box_of) * leaf_dev + within % leaf_dev
                side, chip = (within // leaf_dev) % 2, (within // (2 * leaf_dev)) ^ chip_of
                chip = chip ^ (chip // 2)
                spot = side * (blank // 2) + chip * 3 * leaf_dev + spot
                rows.append(skeletons[jnp.where(j < far_count[leaf], spot, blank)])
            total = total + dot(
                coupling[leaf, :, at * RANK : (at + step) * RANK], jnp.concatenate(rows, axis=0)
            )
        if leaf == 0:
            for load in loads[7:]:
                load.wait()
        out[leaf] = (dot_t(target[leaf], total.astype(BF16)) + near[leaf]).astype(BF16)
        stores += load_all((out.at[leaf],), (out_far.at[leaf],), out_sems.at[pl.ds(leaf, 1)])
    for store in stores:
        store.wait()


def swap(block, axis, first):
    size = lax.axis_size(axis)
    pairs = [(i, i + 1) for i in range(first, size - 1, 2)]
    return lax.ppermute(block, axis, pairs + [(b, a) for a, b in pairs])


def shards(
    densities,
    basis_source,
    basis_target,
    near_blocks,
    near_leaves,
    near_count,
    far_coupling,
    far_leaves,
    far_count,
    leaf_transfer,
    box_transfer,
    box_coupling,
    box_partners,
    top_coupling,
    top_partners,
):
    chips, cores = lax.axis_size("x"), lax.axis_size("core")
    groups = chips * cores
    boxes = lax.axis_size("boxes")
    leaf_dev, points, vectors = densities.shape
    cols, rows = vectors // chips, RANK // cores
    grp = ("x", "core")
    line = ("boxes", "x", "core")

    skeleton, pieces = call(
        functools.partial(upward_body, groups),
        (
            jax.ShapeDtypeStruct((leaf_dev, RANK, vectors), BF16),
            jax.ShapeDtypeStruct((groups, rows, cols), BF16),
        ),
        [HBM] * 3,
        2 * leaf_dev * RANK * vectors * (points + RANK),
        densities.size * 2,
        (
            VMEM(basis_source.shape, BF16),
            VMEM(densities.shape, BF16),
            VMEM(leaf_transfer.shape, BF16),
            pltpu.SemaphoreType.DMA((3,)),
        ),
        WIDE,
    )(basis_source, densities, leaf_transfer)
    arrived = lax.all_to_all(pieces, grp, 0, 0, tiled=True)

    even_skeleton = swap(skeleton, "boxes", 0)
    odd_skeleton = swap(skeleton, "boxes", 1)

    tops = top_partners.T
    sources = box_partners.shape[1] + tops.shape[0] * CHILDREN
    weights = call(
        weight_body,
        jax.ShapeDtypeStruct((RANK, sources * RANK), BF16),
        [HBM, HBM, HBM, SMEM],
        2 * RANK * RANK * RANK * sources,
        box_transfer.size * 2,
        (
            VMEM(box_coupling.shape[1:], BF16),
            VMEM(box_transfer.shape[1:], BF16),
            VMEM(top_coupling.shape[1:], BF16),
            VMEM((tops.shape[0], CHILDREN) + box_transfer.shape[1:], BF16),
            pltpu.SemaphoreType.DMA((3 + tops.shape[0],)),
        ),
        WIDE,
    )(box_coupling, box_transfer, top_coupling, tops)
    spread, trio = call(
        spread_body,
        (
            jax.ShapeDtypeStruct((boxes, rows, cols), BF16),
            jax.ShapeDtypeStruct((3, leaf_dev, RANK, vectors), BF16),
        ),
        [VMEM] * 4 + [pl.ANY],
        groups * rows * cols,
        boxes * rows * cols * 2,
    )(arrived, even_skeleton, skeleton, odd_skeleton, weights)
    all_boxes = lax.all_to_all(spread, "boxes", 0, 0, tiled=True)
    flips = [[(i, i ^ flip) for i in range(chips)] for flip in (1, 3)]
    pair = call(
        pair_body,
        jax.ShapeDtypeStruct((2,) + trio.shape, BF16),
        [VMEM] * 2,
        HUGE,
        4 * trio.size * 2,
    )(trio, lax.ppermute(trio, "x", flips[0]))
    opposite = lax.ppermute(pair, "x", flips[1])

    held, _ = lax.optimization_barrier((densities, pair))
    even = swap(held, line, 0)
    odd = swap(held, line, 1)

    local = call(
        box_body,
        jax.ShapeDtypeStruct((groups, RANK, cols), BF16),
        [VMEM, VMEM, SMEM, SMEM],
        2 * RANK * RANK * sources * cols,
        all_boxes.size * 2,
    )(weights, all_boxes, box_partners, tops)
    local = lax.all_to_all(local, grp, 0, 0, tiled=True)
    mine = call(
        join_body,
        jax.ShapeDtypeStruct((chips,) + trio.shape, BF16),
        [VMEM] * 2 + [pl.ANY] * 3,
        0,
        2 * chips * trio.size * 2,
    )(pair, opposite, local, even, odd)
    other = swap(mine, "core", 0)

    def device_of():
        return (lax.axis_index("boxes") * chips + lax.axis_index("x")) * cores + lax.axis_index("core")

    near_field = call(
        functools.partial(near_body, device_of),
        jax.ShapeDtypeStruct((leaf_dev, points, vectors), F32),
        [HBM] + [pl.ANY] * 5,
        2 * near_blocks.size * vectors,
        near_blocks.size * 2 + 5 * densities.size * 2,
        (
            VMEM(near_blocks.shape, BF16),
            VMEM((3 * leaf_dev + 1, points, vectors), BF16),
            SMEM(near_leaves.shape, jnp.int32),
            SMEM(near_count.shape, jnp.int32),
            VMEM((leaf_dev, points, vectors), F32),
            pltpu.SemaphoreType.DMA((5 + leaf_dev,)),
            pltpu.SemaphoreType.DMA((leaf_dev,)),
        ),
        32 << 20,
        HBM,
    )(near_blocks, even, densities, odd, near_leaves, near_count)
    flat = (chips * 3 * leaf_dev, RANK, vectors)
    return call(
        functools.partial(leaf_body, groups * leaf_dev),
        jax.ShapeDtypeStruct(densities.shape, BF16),
        [HBM] * 4 + [pl.ANY] * 5,
        2 * far_coupling.size * vectors,
        4 * mine.size,
        (
            VMEM(far_coupling.shape, BF16),
            VMEM((cores * flat[0] + 1, RANK, vectors), BF16),
            VMEM(near_field.shape, F32),
            VMEM(leaf_transfer.shape, BF16),
            VMEM(basis_target.shape, BF16),
            SMEM(far_leaves.shape, jnp.int32),
            SMEM(far_count.shape, jnp.int32),
            VMEM(local.shape, BF16),
            VMEM(densities.shape, BF16),
            pltpu.SemaphoreType.DMA((9,)),
            pltpu.SemaphoreType.DMA((leaf_dev,)),
        ),
        32 << 20,
        HBM,
    )(
        far_coupling,
        mine.reshape(flat),
        other.reshape(flat),
        near_field,
        leaf_transfer,
        basis_target,
        far_leaves,
        far_count,
        local,
    )


def solution(mesh):
    boxes, groups = mesh.devices.shape
    fine = Mesh(mesh.devices.reshape(boxes, groups // 2, 2), ("boxes", "x", "core"))
    line = ("boxes", "x", "core")
    leaf = P(line, None, None)
    placed = (
        leaf,
        leaf,
        leaf,
        leaf,
        P(line, None),
        P(line),
        leaf,
        P(line, None),
        P(line),
        leaf,
        P(),
        P("boxes", None, None),
        P("boxes", None),
        P(),
        P(),
    )
    return jax.shard_map(shards, mesh=fine, in_specs=placed, out_specs=leaf, check_vma=False)
```

```python
import functools

import jax
import jax.numpy as jnp
from jax import lax
from jax.experimental import pallas as pl
from jax.experimental.pallas import tpu as pltpu
from jax.sharding import Mesh, PartitionSpec as P

RANK = 64
CHILDREN = 8
F32 = jnp.float32
BF16 = jnp.bfloat16
VMEM = pltpu.VMEM
SMEM = pltpu.SMEM
HBM = pltpu.HBM
WIDE = 119 << 19
HUGE = 10**9


def dot(a, b):
    return jnp.dot(a, b, preferred_element_type=F32)


def dot_t(a, b):
    return lax.dot_general(a, b, (((0,), (0,)), ((), ())), preferred_element_type=F32)


def call(body, out_shape, spaces, flops, moved, scratch=(), limit=16 << 20, out_space=VMEM):
    outs = jax.tree.map(lambda _: pl.BlockSpec(memory_space=out_space), out_shape)
    return pl.pallas_call(
        body,
        out_shape=out_shape,
        in_specs=[pl.BlockSpec(memory_space=s) for s in spaces],
        out_specs=outs,
        scratch_shapes=list(scratch),
        compiler_params=pltpu.CompilerParams(vmem_limit_bytes=limit),
        cost_estimate=pl.CostEstimate(flops=flops, bytes_accessed=moved, transcendentals=0),
    )


def load_all(sources, places, sems):
    loads = [pltpu.make_async_copy(a, b, sems.at[i]) for i, (a, b) in enumerate(zip(sources, places))]
    for load in loads:
        load.start()
    return loads


def upward_body(groups, basis_far, densities_far, transfer_far, skeleton, pieces, basis, densities, transfer, sems):
    for load in load_all((basis_far, densities_far, transfer_far), (basis, densities, transfer), sems):
        load.wait()
    total = None
    for leaf in range(densities.shape[0]):
        value = dot(basis[leaf], densities[leaf]).astype(BF16)
        skeleton[leaf] = value
        term = dot(transfer[leaf], value)
        total = term if total is None else total + term
    total = total.astype(BF16)
    rows, cols = pieces.shape[1:]
    for piece in range(groups):
        top, left = (piece % 2) * rows, (piece // 2) * cols
        pieces[piece] = total[top : top + rows, left : left + cols]


def pair_body(first, second, joined):
    joined[0] = first[...]
    joined[1] = second[...]


def join_body(first, second, after, even, odd, joined):
    half = first.shape[0]
    joined[:half] = first[...]
    joined[half:] = second[...]


def spread_body(arrived, even, own, odd, before, copies, joined):
    joined[0] = even[...]
    joined[1] = own[...]
    joined[2] = odd[...]
    total = arrived[0].astype(F32)
    for piece in range(1, arrived.shape[0]):
        total = total + arrived[piece].astype(F32)
    total = total.astype(BF16)
    for target in range(copies.shape[0]):
        copies[target] = total


def weight_body(coupling_far, transfer_far, top_far, top_partners, weights, coupling, own, row, transfer, sems):
    box = lax.axis_index("boxes")
    half = lax.axis_index("core")
    parent = box // CHILDREN
    slots = top_partners.shape[0]
    sources = [coupling_far.at[0], transfer_far.at[box], top_far.at[parent]]
    sources += [transfer_far.at[pl.ds(top_partners[slot, parent] * CHILDREN, CHILDREN)] for slot in range(slots)]
    loads = load_all(sources, [coupling, own, row] + [transfer.at[slot] for slot in range(slots)], sems)
    for load in loads:
        load.wait()
    lefts = dot_t(own[...], row[...])
    near = coupling.shape[-1]

    def keep(value):
        lane = lax.broadcasted_iota(jnp.int32, value.shape, 1)
        return jnp.where((lane // (RANK // 2)) % 2 == half, value, 0.0).astype(BF16)

    weights[:, :near] = keep(coupling[...].astype(F32))
    span = CHILDREN * RANK
    for slot in range(slots):
        left = lefts[:, slot * RANK : (slot + 1) * RANK].astype(BF16)
        wide = jnp.concatenate([dot(left, transfer[slot, k]) for k in range(CHILDREN)], axis=1)
        weights[:, near + slot * span : near + (slot + 1) * span] = keep(wide)


def box_body(weights, boxes, box_partners, top_partners, copies):
    parent = lax.axis_index("boxes") // CHILDREN
    sources = [box_partners[0, j] for j in range(box_partners.shape[1])]
    for slot in range(top_partners.shape[0]):
        first = top_partners[slot, parent] * CHILDREN
        sources += [first + k for k in range(CHILDREN)]
    total = None
    step = 4
    for at in range(0, len(sources), step):
        rows = []
        for source in sources[at : at + step]:
            value = boxes[source]
            rows += [value, value]
        term = dot(weights[:, at * RANK : (at + step) * RANK], jnp.concatenate(rows, axis=0))
        total = term if total is None else total + term
    total = total.astype(BF16)
    for target in range(copies.shape[0]):
        copies[target] = total


def place(offset, index):
    return jnp.where(index % 2 == 1, offset, 2 - offset)


def near_body(
    device_of, blocks_far, even, own, odd, leaves_far, count_far, out_far, blocks, window, leaves, count, out, sems, out_sems
):
    leaf_dev, points, _ = own.shape
    blank = 3 * leaf_dev
    sources = [leaves_far, count_far, even, own, odd] + [blocks_far.at[leaf] for leaf in range(leaf_dev)]
    places = [leaves, count] + [window.at[pl.ds(i * leaf_dev, leaf_dev)] for i in range(3)]
    loads = load_all(sources, places + [blocks.at[leaf] for leaf in range(leaf_dev)], sems)
    window[blank] = jnp.zeros(window.shape[1:], BF16)
    device = device_of()
    base = (device - 1) * leaf_dev
    for load in loads[:5]:
        load.wait()
    stores = []
    for leaf in range(leaf_dev):
        loads[5 + leaf].wait()
        total = None
        for j in range(leaves.shape[1]):
            source = leaves[leaf, j] - base
            at = place(source // leaf_dev, device) * leaf_dev + source % leaf_dev
            value = window[jnp.where(j < count[leaf], at, blank)]
            term = dot(blocks[leaf, :, j * points : (j + 1) * points], value)
            total = term if total is None else total + term
        out[leaf] = total.astype(BF16)
        stores += load_all((out.at[leaf],), (out_far.at[leaf],), out_sems.at[pl.ds(leaf, 1)])
    for store in stores:
        store.wait()


def leaf_body(
    group_leaves,
    coupling_far,
    mine,
    other,
    near_far,
    transfer_far,
    target_far,
    far_leaves_far,
    far_count_far,
    local_far,
    out_far,
    coupling,
    skeletons,
    near,
    transfer,
    target,
    far_leaves,
    far_count,
    local,
    out,
    sems,
    out_sems,
):
    box_of = lax.axis_index("boxes")
    leaf_dev = transfer.shape[0]
    blank = skeletons.shape[0] - 1
    half = lax.axis_index("core")
    chip_of = lax.axis_index("x")
    loads = load_all(
        (far_leaves_far, far_count_far, local_far, transfer_far, coupling_far, mine, other, target_far, near_far),
        (
            far_leaves,
            far_count,
            local,
            transfer,
            coupling,
            skeletons.at[pl.ds(half * (blank // 2), blank // 2)],
            skeletons.at[pl.ds((1 - half) * (blank // 2), blank // 2)],
            target,
            near,
        ),
        sems,
    )
    skeletons[blank] = jnp.zeros(skeletons.shape[1:], BF16)
    for load in loads[:3]:
        load.wait()
    parts = []
    for piece in range(0, local.shape[0], 2):
        parts.append(local[piece].astype(F32) + local[piece + 1].astype(F32))
    box_local = jnp.concatenate(parts, axis=1).astype(BF16)
    base = (box_of - 1) * group_leaves
    step = 4
    for load in loads[3:7]:
        load.wait()
    stores = []
    for leaf in range(leaf_dev):
        total = dot_t(transfer[leaf], box_local)
        for at in range(0, far_leaves.shape[1], step):
            rows = []
            for j in range(at, at + step):
                source = far_leaves[leaf, j] - base
                within = source % group_leaves
                spot = place(source // group_leaves, box_of) * leaf_dev + within % leaf_dev
                side, chip = (within // leaf_dev) % 2, (within // (2 * leaf_dev)) ^ chip_of
                chip = jnp.where(side == 0, chip, (4 - chip) % 4)
                chip = chip ^ (chip // 2)
                spot = side * (blank // 2) + chip * 3 * leaf_dev + spot
                rows.append(skeletons[jnp.where(j < far_count[leaf], spot, blank)])
            total = total + dot(
                coupling[leaf, :, at * RANK : (at + step) * RANK], jnp.concatenate(rows, axis=0)
            )
        if leaf == 0:
            for load in loads[7:]:
                load.wait()
        out[leaf] = (dot_t(target[leaf], total.astype(BF16)) + near[leaf]).astype(BF16)
        stores += load_all((out.at[leaf],), (out_far.at[leaf],), out_sems.at[pl.ds(leaf, 1)])
    for store in stores:
        store.wait()


def swap(block, axis, first):
    size = lax.axis_size(axis)
    pairs = [(i, i + 1) for i in range(first, size - 1, 2)]
    return lax.ppermute(block, axis, pairs + [(b, a) for a, b in pairs])


def shards(
    densities,
    basis_source,
    basis_target,
    near_blocks,
    near_leaves,
    near_count,
    far_coupling,
    far_leaves,
    far_count,
    leaf_transfer,
    box_transfer,
    box_coupling,
    box_partners,
    top_coupling,
    top_partners,
):
    chips, cores = lax.axis_size("x"), lax.axis_size("core")
    groups = chips * cores
    boxes = lax.axis_size("boxes")
    leaf_dev, points, vectors = densities.shape
    cols, rows = vectors // chips, RANK // cores
    grp = ("x", "core")
    line = ("boxes", "x", "core")

    skeleton, pieces = call(
        functools.partial(upward_body, groups),
        (
            jax.ShapeDtypeStruct((leaf_dev, RANK, vectors), BF16),
            jax.ShapeDtypeStruct((groups, rows, cols), BF16),
        ),
        [HBM] * 3,
        2 * leaf_dev * RANK * vectors * (points + RANK),
        densities.size * 2,
        (
            VMEM(basis_source.shape, BF16),
            VMEM(densities.shape, BF16),
            VMEM(leaf_transfer.shape, BF16),
            pltpu.SemaphoreType.DMA((3,)),
        ),
        WIDE,
    )(basis_source, densities, leaf_transfer)
    arrived = lax.all_to_all(pieces, grp, 0, 0, tiled=True)

    even_skeleton = swap(skeleton, "boxes", 0)
    odd_skeleton = swap(skeleton, "boxes", 1)

    tops = top_partners.T
    sources = box_partners.shape[1] + tops.shape[0] * CHILDREN
    weights = call(
        weight_body,
        jax.ShapeDtypeStruct((RANK, sources * RANK), BF16),
        [HBM, HBM, HBM, SMEM],
        2 * RANK * RANK * RANK * sources,
        box_transfer.size * 2,
        (
            VMEM(box_coupling.shape[1:], BF16),
            VMEM(box_transfer.shape[1:], BF16),
            VMEM(top_coupling.shape[1:], BF16),
            VMEM((tops.shape[0], CHILDREN) + box_transfer.shape[1:], BF16),
            pltpu.SemaphoreType.DMA((3 + tops.shape[0],)),
        ),
        WIDE,
    )(box_coupling, box_transfer, top_coupling, tops)
    spread, trio = call(
        spread_body,
        (
            jax.ShapeDtypeStruct((boxes, rows, cols), BF16),
            jax.ShapeDtypeStruct((3, leaf_dev, RANK, vectors), BF16),
        ),
        [VMEM] * 4 + [pl.ANY],
        groups * rows * cols,
        boxes * rows * cols * 2,
    )(arrived, even_skeleton, skeleton, odd_skeleton, weights)
    all_boxes = lax.all_to_all(spread, "boxes", 0, 0, tiled=True)
    ring = [(chip, core) for chip in range(chips) for core in range(cores)]
    flips = [
        [(chip * cores + core, (chip ^ flip[core]) * cores + core) for chip, core in ring]
        for flip in ((1, 3), (3, 1))
    ]
    pair = call(
        pair_body,
        jax.ShapeDtypeStruct((2,) + trio.shape, BF16),
        [VMEM] * 2,
        HUGE,
        4 * trio.size * 2,
    )(trio, lax.ppermute(trio, grp, flips[0]))
    opposite = lax.ppermute(pair, grp, flips[1])

    held, _ = lax.optimization_barrier((densities, pair))
    even = swap(held, line, 0)
    odd = swap(held, line, 1)

    local = call(
        box_body,
        jax.ShapeDtypeStruct((groups, RANK, cols), BF16),
        [VMEM, VMEM, SMEM, SMEM],
        2 * RANK * RANK * sources * cols,
        all_boxes.size * 2,
    )(weights, all_boxes, box_partners, tops)
    local = lax.all_to_all(local, grp, 0, 0, tiled=True)
    mine = call(
        join_body,
        jax.ShapeDtypeStruct((chips,) + trio.shape, BF16),
        [VMEM] * 2 + [pl.ANY] * 3,
        0,
        2 * chips * trio.size * 2,
    )(pair, opposite, local, even, odd)
    other = swap(mine, "core", 0)

    def device_of():
        return (lax.axis_index("boxes") * chips + lax.axis_index("x")) * cores + lax.axis_index("core")

    near_field = call(
        functools.partial(near_body, device_of),
        jax.ShapeDtypeStruct((leaf_dev, points, vectors), BF16),
        [HBM] + [pl.ANY] * 5,
        2 * near_blocks.size * vectors,
        near_blocks.size * 2 + 5 * densities.size * 2,
        (
            VMEM(near_blocks.shape, BF16),
            VMEM((3 * leaf_dev + 1, points, vectors), BF16),
            SMEM(near_leaves.shape, jnp.int32),
            SMEM(near_count.shape, jnp.int32),
            VMEM((leaf_dev, points, vectors), BF16),
            pltpu.SemaphoreType.DMA((5 + leaf_dev,)),
            pltpu.SemaphoreType.DMA((leaf_dev,)),
        ),
        16 << 20,
        HBM,
    )(near_blocks, even, densities, odd, near_leaves, near_count)
    flat = (chips * 3 * leaf_dev, RANK, vectors)
    return call(
        functools.partial(leaf_body, groups * leaf_dev),
        jax.ShapeDtypeStruct(densities.shape, BF16),
        [HBM] * 4 + [pl.ANY] * 5,
        2 * far_coupling.size * vectors,
        4 * mine.size,
        (
            VMEM(far_coupling.shape, BF16),
            VMEM((cores * flat[0] + 1, RANK, vectors), BF16),
            VMEM(near_field.shape, BF16),
            VMEM(leaf_transfer.shape, BF16),
            VMEM(basis_target.shape, BF16),
            SMEM(far_leaves.shape, jnp.int32),
            SMEM(far_count.shape, jnp.int32),
            VMEM(local.shape, BF16),
            VMEM(densities.shape, BF16),
            pltpu.SemaphoreType.DMA((9,)),
            pltpu.SemaphoreType.DMA((leaf_dev,)),
        ),
        16 << 20,
        HBM,
    )(
        far_coupling,
        mine.reshape(flat),
        other.reshape(flat),
        near_field,
        leaf_transfer,
        basis_target,
        far_leaves,
        far_count,
        local,
    )


def solution(mesh):
    boxes, groups = mesh.devices.shape
    fine = Mesh(mesh.devices.reshape(boxes, groups // 2, 2), ("boxes", "x", "core"))
    line = ("boxes", "x", "core")
    leaf = P(line, None, None)
    placed = (
        leaf,
        leaf,
        leaf,
        leaf,
        P(line, None),
        P(line),
        leaf,
        P(line, None),
        P(line),
        leaf,
        P(),
        P("boxes", None, None),
        P("boxes", None),
        P(),
        P(),
    )
    return jax.shard_map(shards, mesh=fine, in_specs=placed, out_specs=leaf, check_vma=False)
```
